32 devices in a mesh: rep: 2 (over x), region: 2 (over core), dev: 8 (over z, y).
Axes of the slice: x: 2, y: 2, z: 4, core: 2. Of those that a mesh axis runs over, the one named last changes fastest.
Arguments:
- queries: bfloat16 [32768, 512], P(('rep', 'region', 'dev')), parts along dimension 0, may hold values from -6 to 6
- tiles: bfloat16 [64, 1024, 1024], P(('rep', 'region', 'dev')), parts along dimension 0, may hold values from -0.09375 to 0.09375
- tile_cols: int32 [32, 2], P(('rep', 'region', 'dev')), parts along dimension 0, may hold values from 0 to 15, as said below
- tile_count: int32 [32], P(('rep', 'region', 'dev')), parts along dimension 0, may hold values from 1 to 2, as said below
Outputs:
- ranking: float32 [32768, 512], P(('rep', 'region', 'dev')), parts along dimension 0
The draws below stay inside these ranges and needn't reach their ends.
There are 2 independent parts, one for each index of `rep`. The reference program is written for one: setup_inputs(seed, part) draws one part's arguments, and reference() takes and returns one part's arrays. A program takes and returns all parts, laid end to end along the dimension named above; each array names one. Nothing has to cross between parts.
Inputs may be any that keep to these rules, and one draw needn't show every extreme that they name: For row block r, tile_cols[r, s] is r, or r + k with 1 <= k <= 2 inside the same group of 8 blocks, or r + 8 when r < 8. `tile_count`: some row block has all 2 slots live in every draw.
All inputs are finite; a program needn't handle non-finite values.
Results may differ from the reference program's by a relative error of at most 0.002.
Values may be sent and summed in bfloat16 or wider, within the bound.
A program may use at most 128 MiB of HBM per device.

```python
import jax
import jax.numpy as jnp
from jax import lax

TILE = 1024
QCOLS = 512
ITERS = 3
REACH = 2
CAP = 2
BLOCKS = 16
N_DEV = 8


def draw_tile_cols(key, part):
    blocks = jnp.arange(BLOCKS, dtype=jnp.int32)[:, None]
    option = jax.random.randint(key, (BLOCKS, CAP), 0, REACH + 2).astype(jnp.int32)
    local = blocks % N_DEV
    region_of = blocks // N_DEV
    fits = (option <= REACH) & (local + option < N_DEV)
    cross = (option == REACH + 1) & (region_of == 0)
    chosen = jnp.where(fits, blocks + option, jnp.where(cross, blocks + N_DEV, blocks))
    return chosen.astype(jnp.int32)


def draw_tile_count(key, part):
    first, second = jax.random.split(jax.random.fold_in(key, 7))
    counts = jax.random.randint(first, (BLOCKS,), 1, CAP + 1).astype(jnp.int32)
    fullest = jax.random.randint(second, (), 0, BLOCKS).astype(jnp.int32)
    return jnp.where(jnp.arange(BLOCKS, dtype=jnp.int32) == fullest, CAP, counts).astype(jnp.int32)


def levels(key, dims, shards, low, high):
    loudness = 1.0
    for position, parts in shards:
        heights = jax.random.uniform(jax.random.fold_in(jax.random.fold_in(key, 6), position), (parts,), jnp.float32, low / len(shards), high / len(shards))
        loudness = loudness * jnp.repeat(jnp.exp(heights), dims[position] // parts).reshape((-1,) + (1,) * (len(dims) - 1 - position))
    return loudness


def bell_draw(key, extent, scale, most, cuts=(), held_as=jnp.bfloat16):
    level = levels(key, extent, cuts, -0.22, 0.18) if cuts else 1.0
    array = jax.random.normal(key, extent, jnp.float32) * scale * level
    return jnp.minimum(jnp.maximum(array, -most), most).astype(held_as)


def setup_inputs(seed: int = 0, part: int = 0) -> dict:
    seeds = jax.random.split(jax.random.key(seed), 5)
    own_keys = jax.random.split(jax.random.fold_in(seeds[4], part), 5)
    return {
        "queries": bell_draw(own_keys[0], (BLOCKS * TILE, QCOLS), 1.0, 6.0, ((0, 16),)),
        "tiles": bell_draw(own_keys[1], (BLOCKS * CAP, TILE, TILE), (TILE * (REACH + 2)) ** -0.5, 0.09375, ((0, 16),)),
        "tile_cols": draw_tile_cols(jax.random.fold_in(jax.random.fold_in(seeds[4], part), 71), part),
        "tile_count": draw_tile_count(jax.random.fold_in(jax.random.fold_in(seeds[4], part), 71), part),
    }


damping = 0.8


def reference(queries, tiles, tile_cols, tile_count):
    anchor = queries.astype(jnp.float32)
    field = queries
    row_list = jnp.repeat(jnp.arange(BLOCKS, dtype=jnp.int32), CAP)
    col_list = tile_cols.reshape(-1).astype(jnp.int32)
    live_list = (jnp.arange(CAP, dtype=jnp.int32)[None, :] < tile_count[:, None]).reshape(-1)
    update = anchor
    for iteration in range(ITERS):
        blocked = field.reshape(BLOCKS, TILE, QCOLS)

        def visit(total, item):
            tile_now, row_block, col_block, alive = item
            source = lax.dynamic_index_in_dim(blocked, col_block, 0, keepdims=False)
            own = lax.dynamic_index_in_dim(blocked, row_block, 0, keepdims=False)
            forward = jnp.dot(tile_now, source, preferred_element_type=jnp.float32)
            backward = lax.dot_general(tile_now, own, (((0,), (0,)), ((), ())), preferred_element_type=jnp.float32)
            forward = jnp.where(alive, forward, jnp.zeros_like(forward))
            backward = jnp.where(alive & (col_block != row_block), backward, jnp.zeros_like(backward))
            total = total.at[row_block].add(forward)
            total = total.at[col_block].add(backward)
            return total, None

        start = jnp.zeros((BLOCKS, TILE, QCOLS), jnp.float32)
        total, unused = lax.scan(visit, start, (tiles, row_list, col_list, live_list))
        update = damping * total.reshape(BLOCKS * TILE, QCOLS) + anchor
        field = update.astype(jnp.bfloat16)
    return update
```

```python
import functools

import jax
import jax.numpy as jnp
from jax import lax
from jax.experimental import pallas as pl
from jax.experimental.pallas import tpu as pltpu
from jax.sharding import PartitionSpec as P

ITERS = 3
REACH = 2
CHUNKS = 2
ROWS = 256
KINDS = REACH + 1

damping = 0.8

MESH = pl.DeviceIdType.MESH


def kernel(n, bins_ref, gates_ref, tiles_ref, q_ref, out_ref, *scratch):
    slots, tile, _ = tiles_ref.shape
    width = q_ref.shape[1] // CHUNKS
    steps = ITERS * CHUNKS
    wt_ref = scratch[0]
    srcs = scratch[1 : 1 + steps]
    gots = scratch[1 + steps : 1 + 2 * steps]
    puts = scratch[1 + 2 * steps : 1 + 3 * steps]
    send_sem, recv_sem = scratch[1 + 3 * steps :]

    rep = lax.axis_index("rep")
    region = lax.axis_index("region")
    me = lax.axis_index("dev")

    has_lower = [me >= d for d in range(1, REACH + 1)] + [region == 1]
    has_upper = [me + d < n for d in range(1, REACH + 1)] + [region == 0]
    lower = [(rep, region, me - d) for d in range(1, REACH + 1)] + [(rep, 0, me)]
    upper = [(rep, region, me + d) for d in range(1, REACH + 1)] + [(rep, 1, me)]

    barrier = pltpu.get_barrier_semaphore()
    count = jnp.int32(0)
    for there, device in list(zip(has_lower, lower)) + list(zip(has_upper, upper)):
        count = count + there.astype(jnp.int32)

        @pl.when(there)
        def _(device=device):
            pl.semaphore_signal(barrier, inc=1, device_id=device, device_id_type=MESH)

    for ch in range(CHUNKS):
        srcs[ch][0] = q_ref[:, ch * width : (ch + 1) * width]
    pl.semaphore_wait(barrier, count)

    def field_copy(step, k, device):
        return pltpu.make_async_remote_copy(
            src_ref=srcs[step].at[0],
            dst_ref=srcs[step].at[k + 1],
            send_sem=send_sem.at[step, k],
            recv_sem=recv_sem.at[step, k],
            device_id=device,
            device_id_type=MESH,
        )

    def product_copy(step, k, device):
        return pltpu.make_async_remote_copy(
            src_ref=puts[step].at[k],
            dst_ref=gots[step].at[k],
            send_sem=send_sem.at[step, KINDS + k],
            recv_sem=recv_sem.at[step, KINDS + k],
            device_id=device,
            device_id_type=MESH,
        )

    def send_fields(step):
        for k in range(KINDS):

            @pl.when(has_lower[k])
            def _(k=k):
                field_copy(step, k, lower[k]).start()

    def send_products(step):
        source = srcs[step]

        @pl.loop(0, tile // ROWS)
        def _(i):
            rows = pl.ds(pl.multiple_of(i * ROWS, ROWS), ROWS)
            parts = [
                jnp.dot(wt_ref[s, rows, :], source[0], preferred_element_type=jnp.float32)
                for s in range(slots)
            ]
            for k in range(KINDS):
                total = gates_ref[0, k + 1] * parts[0]
                for s in range(1, slots):
                    total = total + gates_ref[s, k + 1] * parts[s]
                puts[step][k, rows, :] = total.astype(jnp.bfloat16)

        for k in range(KINDS):

            @pl.when(has_upper[k])
            def _(k=k):
                product_copy(step, k, upper[k]).start()

    def finish(step):
        for k in range(KINDS):

            @pl.when(has_upper[k])
            def _(k=k):
                field_copy(step, k, upper[k]).wait_recv()

            @pl.when(has_lower[k])
            def _(k=k):
                product_copy(step, k, lower[k]).wait_recv()

        it, ch = divmod(step, CHUNKS)
        columns = pl.ds(ch * width, width)
        source = srcs[step]

        @pl.loop(0, tile // ROWS)
        def _(i):
            rows = pl.ds(pl.multiple_of(i * ROWS, ROWS), ROWS)
            total = jnp.zeros((ROWS, width), jnp.float32)
            for s in range(slots):
                live = gates_ref[s, KINDS + 1]
                total = total + live * jnp.dot(
                    tiles_ref[s, rows, :], source[bins_ref[s]], preferred_element_type=jnp.float32
                )
            for k in range(KINDS):
                landed = gots[step][k, rows, :].astype(jnp.float32)
                total = total + jnp.where(has_lower[k], landed, jnp.zeros_like(landed))
            update = damping * total + q_ref[rows, columns].astype(jnp.float32)
            if it == ITERS - 1:
                out_ref[rows, columns] = update
            else:
                srcs[step + CHUNKS][0, rows, :] = update.astype(jnp.bfloat16)

    for ch in range(CHUNKS):
        send_fields(ch)

    for s in range(slots):

        @pl.loop(0, tile // ROWS)
        def _(i, s=s):
            rows = pl.ds(pl.multiple_of(i * ROWS, ROWS), ROWS)
            wt_ref[s, rows, :] = tiles_ref[s, :, rows].T

    for ch in range(CHUNKS):
        send_products(ch)

    for step in range(steps):
        finish(step)
        if step + CHUNKS < steps:
            send_fields(step + CHUNKS)
            send_products(step + CHUNKS)

    for step in range(steps):
        for k in range(KINDS):

            @pl.when(has_lower[k])
            def _(step=step, k=k):
                field_copy(step, k, lower[k]).wait_send()

            @pl.when(has_upper[k])
            def _(step=step, k=k):
                product_copy(step, k, upper[k]).wait_send()


def on_device(queries, tiles, tile_cols, tile_count):
    n = lax.axis_size("dev")
    slots, tile, _ = tiles.shape
    cols = queries.shape[1]
    width = cols // CHUNKS
    steps = ITERS * CHUNKS
    own = lax.axis_index("region") * n + lax.axis_index("dev")
    distance = tile_cols[0] - own
    alive = jnp.arange(slots, dtype=jnp.int32) < tile_count[0]
    bins = jnp.where(distance > REACH, REACH + 1, distance)
    bins = jnp.where(alive, bins, 0).astype(jnp.int32)
    which = (bins[:, None] == jnp.arange(REACH + 2, dtype=jnp.int32)[None]) & alive[:, None]
    gates = jnp.concatenate([which, alive[:, None]], 1).astype(jnp.float32)

    vmem = pl.BlockSpec(memory_space=pltpu.VMEM)
    smem = pl.BlockSpec(memory_space=pltpu.SMEM)
    products = 2 * slots * ITERS
    return pl.pallas_call(
        functools.partial(kernel, n),
        out_shape=jax.ShapeDtypeStruct((tile, cols), jnp.float32),
        in_specs=[smem, smem, vmem, vmem],
        out_specs=vmem,
        scratch_shapes=[pltpu.VMEM((slots, tile, tile), jnp.bfloat16)]
        + [pltpu.VMEM((KINDS + 1, tile, width), jnp.bfloat16)] * steps
        + [pltpu.VMEM((KINDS, tile, width), jnp.bfloat16)] * (2 * steps)
        + [pltpu.SemaphoreType.DMA((steps, 2 * KINDS))] * 2,
        compiler_params=pltpu.CompilerParams(
            collective_id=0, has_side_effects=True, vmem_limit_bytes=58 * 2**20
        ),
        cost_estimate=pl.CostEstimate(
            flops=2 * products * tile * tile * cols,
            bytes_accessed=2 * tiles.size + 6 * tile * cols,
            transcendentals=0,
        ),
        name="diffuse",
    )(bins, gates, tiles, queries)


def solution(mesh):
    return jax.shard_map(
        on_device,
        mesh=mesh,
        in_specs=(
            P(("rep", "region", "dev"), None),
            P(("rep", "region", "dev"), None, None),
            P(("rep", "region", "dev"), None),
            P(("rep", "region", "dev")),
        ),
        out_specs=P(("rep", "region", "dev"), None),
        check_vma=False,
    )
```

```python
import functools

import jax
import jax.numpy as jnp
from jax import lax
from jax.experimental import pallas as pl
from jax.experimental.pallas import tpu as pltpu
from jax.sharding import PartitionSpec as P

ITERS = 3
REACH = 2
CHUNKS = 2
ROWS = 256
KINDS = REACH + 1

damping = 0.8

MESH = pl.DeviceIdType.MESH


def kernel(n, cols_ref, count_ref, tiles_hbm, q_ref, out_ref, *scratch):
    slots, tile, _ = tiles_hbm.shape
    width = q_ref.shape[1] // CHUNKS
    steps = ITERS * CHUNKS
    tiles_ref, wt_ref = scratch[:2]
    srcs = scratch[2 : 2 + steps]
    gots = scratch[2 + steps : 2 + 2 * steps]
    puts = scratch[2 + 2 * steps : 2 + 3 * steps]
    send_sem, recv_sem, tile_sem = scratch[2 + 3 * steps :]
    fetches = [
        pltpu.make_async_copy(tiles_hbm.at[s], tiles_ref.at[s], tile_sem.at[s])
        for s in range(slots)
    ]

    rep = lax.axis_index("rep")
    region = lax.axis_index("region")
    me = lax.axis_index("dev")

    bins, gates = [], []
    for s in range(slots):
        distance = cols_ref[0, s] - (region * n + me)
        live = s < count_ref[0]
        place = jnp.where(distance > REACH, REACH + 1, distance)
        bins.append(jnp.where(live, place, 0))
        alive = jnp.where(live, 1.0, 0.0).astype(jnp.float32)
        gates.append([jnp.where(place == k, alive, 0.0) for k in range(KINDS + 1)] + [alive])

    has_lower = [me >= d for d in range(1, REACH + 1)] + [region == 1]
    has_upper = [me + d < n for d in range(1, REACH + 1)] + [region == 0]
    lower = [(rep, region, me - d) for d in range(1, REACH + 1)] + [(rep, 0, me)]
    upper = [(rep, region, me + d) for d in range(1, REACH + 1)] + [(rep, 1, me)]

    for fetch in fetches:
        fetch.start()

    barrier = pltpu.get_barrier_semaphore()
    count = jnp.int32(0)
    for there, device in list(zip(has_lower, lower)) + list(zip(has_upper, upper)):
        count = count + there.astype(jnp.int32)

        @pl.when(there)
        def _(device=device):
            pl.semaphore_signal(barrier, inc=1, device_id=device, device_id_type=MESH)

    for ch in range(CHUNKS):
        srcs[ch][0] = q_ref[:, ch * width : (ch + 1) * width]
    pl.semaphore_wait(barrier, count)

    def field_copy(step, k, device):
        return pltpu.make_async_remote_copy(
            src_ref=srcs[step].at[0],
            dst_ref=srcs[step].at[k + 1],
            send_sem=send_sem.at[step, k],
            recv_sem=recv_sem.at[step, k],
            device_id=device,
            device_id_type=MESH,
        )

    def product_copy(step, k, device):
        return pltpu.make_async_remote_copy(
            src_ref=puts[step].at[k],
            dst_ref=gots[step].at[k],
            send_sem=send_sem.at[step, KINDS + k],
            recv_sem=recv_sem.at[step, KINDS + k],
            device_id=device,
            device_id_type=MESH,
        )

    def send_fields(step):
        for k in range(KINDS):

            @pl.when(has_lower[k])
            def _(k=k):
                field_copy(step, k, lower[k]).start()

    def send_products(step):
        source = srcs[step]

        @pl.loop(0, tile // ROWS)
        def _(i):
            rows = pl.ds(pl.multiple_of(i * ROWS, ROWS), ROWS)
            parts = [
                jnp.dot(wt_ref[s, rows, :], source[0], preferred_element_type=jnp.float32)
                for s in range(slots)
            ]
            for k in range(KINDS):
                total = gates[0][k + 1] * parts[0]
                for s in range(1, slots):
                    total = total + gates[s][k + 1] * parts[s]
                puts[step][k, rows, :] = total.astype(jnp.bfloat16)

        for k in range(KINDS):

            @pl.when(has_upper[k])
            def _(k=k):
                product_copy(step, k, upper[k]).start()

    def finish(step):
        for k in range(KINDS):

            @pl.when(has_upper[k])
            def _(k=k):
                field_copy(step, k, upper[k]).wait_recv()

            @pl.when(has_lower[k])
            def _(k=k):
                product_copy(step, k, lower[k]).wait_recv()

        it, ch = divmod(step, CHUNKS)
        columns = pl.ds(ch * width, width)
        source = srcs[step]

        @pl.loop(0, tile // ROWS)
        def _(i):
            rows = pl.ds(pl.multiple_of(i * ROWS, ROWS), ROWS)
            total = jnp.zeros((ROWS, width), jnp.float32)
            for s in range(slots):
                live = gates[s][KINDS + 1]
                total = total + live * jnp.dot(
                    tiles_ref[s, rows, :], source[bins[s]], preferred_element_type=jnp.float32
                )
            for k in range(KINDS):
                landed = gots[step][k, rows, :].astype(jnp.float32)
                total = total + jnp.where(has_lower[k], landed, jnp.zeros_like(landed))
            update = damping * total + q_ref[rows, columns].astype(jnp.float32)
            if it == ITERS - 1:
                out_ref[rows, columns] = update
            else:
                srcs[step + CHUNKS][0, rows, :] = update.astype(jnp.bfloat16)

    for ch in range(CHUNKS):
        send_fields(ch)

    for s in range(slots):
        fetches[s].wait()

        @pl.loop(0, tile // ROWS)
        def _(i, s=s):
            rows = pl.ds(pl.multiple_of(i * ROWS, ROWS), ROWS)
            wt_ref[s, rows, :] = tiles_ref[s, :, rows].T

    for ch in range(CHUNKS):
        send_products(ch)

    for step in range(steps):
        finish(step)
        if step + CHUNKS < steps:
            send_fields(step + CHUNKS)
            send_products(step + CHUNKS)

    for step in range(steps):
        for k in range(KINDS):

            @pl.when(has_lower[k])
            def _(step=step, k=k):
                field_copy(step, k, lower[k]).wait_send()

            @pl.when(has_upper[k])
            def _(step=step, k=k):
                product_copy(step, k, upper[k]).wait_send()


def on_device(queries, tiles, tile_cols, tile_count):
    n = lax.axis_size("dev")
    slots, tile, _ = tiles.shape
    cols = queries.shape[1]
    width = cols // CHUNKS
    steps = ITERS * CHUNKS
    vmem = pl.BlockSpec(memory_space=pltpu.VMEM)
    smem = pl.BlockSpec(memory_space=pltpu.SMEM)
    products = 2 * slots * ITERS
    return pl.pallas_call(
        functools.partial(kernel, n),
        out_shape=jax.ShapeDtypeStruct((tile, cols), jnp.float32),
        in_specs=[smem, smem, pl.BlockSpec(memory_space=pl.ANY), vmem],
        out_specs=vmem,
        scratch_shapes=[pltpu.VMEM((slots, tile, tile), jnp.bfloat16)] * 2
        + [pltpu.VMEM((KINDS + 1, tile, width), jnp.bfloat16)] * steps
        + [pltpu.VMEM((KINDS, tile, width), jnp.bfloat16)] * (2 * steps)
        + [pltpu.SemaphoreType.DMA((steps, 2 * KINDS))] * 2
        + [pltpu.SemaphoreType.DMA((slots,))],
        compiler_params=pltpu.CompilerParams(
            collective_id=0, has_side_effects=True, vmem_limit_bytes=58 * 2**20
        ),
        cost_estimate=pl.CostEstimate(
            flops=2 * products * tile * tile * cols,
            bytes_accessed=2 * tiles.size + 6 * tile * cols,
            transcendentals=0,
        ),
        name="diffuse",
    )(tile_cols, tile_count, tiles, queries)


def solution(mesh):
    return jax.shard_map(
        on_device,
        mesh=mesh,
        in_specs=(
            P(("rep", "region", "dev"), None),
            P(("rep", "region", "dev"), None, None),
            P(("rep", "region", "dev"), None),
            P(("rep", "region", "dev")),
        ),
        out_specs=P(("rep", "region", "dev"), None),
        check_vma=False,
    )
```

```python
import functools

import jax
import jax.numpy as jnp
from jax import lax
from jax.experimental import pallas as pl
from jax.experimental.pallas import tpu as pltpu
from jax.sharding import PartitionSpec as P

ITERS = 3
REACH = 2
CHUNKS = 2
ROWS = 256
KINDS = REACH + 1

damping = 0.8

MESH = pl.DeviceIdType.MESH


def kernel(n, cols_ref, count_ref, tiles_hbm, q_ref, out_hbm, *scratch):
    slots, tile, _ = tiles_hbm.shape
    width = q_ref.shape[1] // CHUNKS
    steps = ITERS * CHUNKS
    tiles_ref, wt_ref = scratch[:2]
    srcs = scratch[2 : 2 + steps]
    gots = scratch[2 + steps : 2 + 2 * steps]
    puts = scratch[2 + 2 * steps : 2 + 3 * steps]
    sums = scratch[2 + 3 * steps : 2 + 3 * steps + CHUNKS]
    send_sem, recv_sem, tile_sem, out_sem = scratch[2 + 3 * steps + CHUNKS :]
    fetches = [
        pltpu.make_async_copy(tiles_hbm.at[s], tiles_ref.at[s], tile_sem.at[s])
        for s in range(slots)
    ]

    rep = lax.axis_index("rep")
    region = lax.axis_index("region")
    me = lax.axis_index("dev")

    bins, gates = [], []
    for s in range(slots):
        distance = cols_ref[0, s] - (region * n + me)
        live = s < count_ref[0]
        place = jnp.where(distance > REACH, REACH + 1, distance)
        bins.append(jnp.where(live, place, 0))
        alive = jnp.where(live, 1.0, 0.0).astype(jnp.float32)
        gates.append([jnp.where(place == k, alive, 0.0) for k in range(KINDS + 1)] + [alive])

    has_lower = [me >= d for d in range(1, REACH + 1)] + [region == 1]
    has_upper = [me + d < n for d in range(1, REACH + 1)] + [region == 0]
    lower = [(rep, region, me - d) for d in range(1, REACH + 1)] + [(rep, 0, me)]
    upper = [(rep, region, me + d) for d in range(1, REACH + 1)] + [(rep, 1, me)]

    for fetch in fetches:
        fetch.start()

    barrier = pltpu.get_barrier_semaphore()
    count = jnp.int32(0)
    for there, device in list(zip(has_lower, lower)) + list(zip(has_upper, upper)):
        count = count + there.astype(jnp.int32)

        @pl.when(there)
        def _(device=device):
            pl.semaphore_signal(barrier, inc=1, device_id=device, device_id_type=MESH)

    for ch in range(CHUNKS):
        srcs[ch][0] = q_ref[:, ch * width : (ch + 1) * width]
    pl.semaphore_wait(barrier, count)

    def field_copy(step, k, device):
        return pltpu.make_async_remote_copy(
            src_ref=srcs[step].at[0],
            dst_ref=srcs[step].at[k + 1],
            send_sem=send_sem.at[step, k],
            recv_sem=recv_sem.at[step, k],
            device_id=device,
            device_id_type=MESH,
        )

    def product_copy(step, k, device):
        return pltpu.make_async_remote_copy(
            src_ref=puts[step].at[k],
            dst_ref=gots[step].at[k],
            send_sem=send_sem.at[step, KINDS + k],
            recv_sem=recv_sem.at[step, KINDS + k],
            device_id=device,
            device_id_type=MESH,
        )

    def send_fields(step):
        for k in range(KINDS):

            @pl.when(has_lower[k])
            def _(k=k):
                field_copy(step, k, lower[k]).start()

    def send_products(step):
        source = srcs[step]

        @pl.loop(0, tile // ROWS)
        def _(i):
            rows = pl.ds(pl.multiple_of(i * ROWS, ROWS), ROWS)
            parts = [
                jnp.dot(wt_ref[s, rows, :], source[0], preferred_element_type=jnp.float32)
                for s in range(slots)
            ]
            for k in range(KINDS):
                total = gates[0][k + 1] * parts[0]
                for s in range(1, slots):
                    total = total + gates[s][k + 1] * parts[s]
                puts[step][k, rows, :] = total.astype(jnp.bfloat16)

        for k in range(KINDS):

            @pl.when(has_upper[k])
            def _(k=k):
                product_copy(step, k, upper[k]).start()

    def result_copy(ch):
        return pltpu.make_async_copy(
            sums[ch], out_hbm.at[:, pl.ds(ch * width, width)], out_sem.at[ch]
        )

    def finish(step):
        it, ch = divmod(step, CHUNKS)
        columns = pl.ds(ch * width, width)
        source = srcs[step]

        for k in range(KINDS):

            @pl.when(has_upper[k])
            def _(k=k):
                field_copy(step, k, upper[k]).wait_recv()

        @pl.loop(0, tile // ROWS)
        def _(i):
            rows = pl.ds(pl.multiple_of(i * ROWS, ROWS), ROWS)
            total = jnp.zeros((ROWS, width), jnp.float32)
            for s in range(slots):
                live = gates[s][KINDS + 1]
                total = total + live * jnp.dot(
                    tiles_ref[s, rows, :], source[bins[s]], preferred_element_type=jnp.float32
                )
            sums[ch][rows, :] = total

        for k in range(KINDS):

            @pl.when(has_lower[k])
            def _(k=k):
                product_copy(step, k, lower[k]).wait_recv()

        @pl.loop(0, tile // ROWS)
        def _(i):
            rows = pl.ds(pl.multiple_of(i * ROWS, ROWS), ROWS)
            total = sums[ch][rows, :]
            for k in range(KINDS):
                landed = gots[step][k, rows, :].astype(jnp.float32)
                total = total + jnp.where(has_lower[k], landed, jnp.zeros_like(landed))
            update = damping * total + q_ref[rows, columns].astype(jnp.float32)
            if it == ITERS - 1:
                sums[ch][rows, :] = update
            else:
                srcs[step + CHUNKS][0, rows, :] = update.astype(jnp.bfloat16)

        if it == ITERS - 1:
            result_copy(ch).start()

    for ch in range(CHUNKS):
        send_fields(ch)

    for s in range(slots):
        fetches[s].wait()

        @pl.loop(0, tile // ROWS)
        def _(i, s=s):
            rows = pl.ds(pl.multiple_of(i * ROWS, ROWS), ROWS)
            wt_ref[s, rows, :] = tiles_ref[s, :, rows].T

    for ch in range(CHUNKS):
        send_products(ch)

    for step in range(steps):
        finish(step)
        if step + CHUNKS < steps:
            send_fields(step + CHUNKS)
            send_products(step + CHUNKS)

    for step in range(steps):
        for k in range(KINDS):

            @pl.when(has_lower[k])
            def _(step=step, k=k):
                field_copy(step, k, lower[k]).wait_send()

            @pl.when(has_upper[k])
            def _(step=step, k=k):
                product_copy(step, k, upper[k]).wait_send()

    for ch in range(CHUNKS):
        result_copy(ch).wait()


def on_device(queries, tiles, tile_cols, tile_count):
    n = lax.axis_size("dev")
    slots, tile, _ = tiles.shape
    cols = queries.shape[1]
    width = cols // CHUNKS
    steps = ITERS * CHUNKS
    vmem = pl.BlockSpec(memory_space=pltpu.VMEM)
    smem = pl.BlockSpec(memory_space=pltpu.SMEM)
    products = 2 * slots * ITERS
    return pl.pallas_call(
        functools.partial(kernel, n),
        out_shape=jax.ShapeDtypeStruct((tile, cols), jnp.float32),
        in_specs=[smem, smem, pl.BlockSpec(memory_space=pl.ANY), vmem],
        out_specs=pl.BlockSpec(memory_space=pl.ANY),
        scratch_shapes=[pltpu.VMEM((slots, tile, tile), jnp.bfloat16)] * 2
        + [pltpu.VMEM((KINDS + 1, tile, width), jnp.bfloat16)] * steps
        + [pltpu.VMEM((KINDS, tile, width), jnp.bfloat16)] * (2 * steps)
        + [pltpu.VMEM((tile, width), jnp.float32)] * CHUNKS
        + [pltpu.SemaphoreType.DMA((steps, 2 * KINDS))] * 2
        + [pltpu.SemaphoreType.DMA((slots,)), pltpu.SemaphoreType.DMA((CHUNKS,))],
        compiler_params=pltpu.CompilerParams(
            collective_id=0, has_side_effects=True, vmem_limit_bytes=58 * 2**20
        ),
        cost_estimate=pl.CostEstimate(
            flops=2 * products * tile * tile * cols,
            bytes_accessed=2 * tiles.size + 6 * tile * cols,
            transcendentals=0,
        ),
        name="diffuse",
    )(tile_cols, tile_count, tiles, queries)


def solution(mesh):
    return jax.shard_map(
        on_device,
        mesh=mesh,
        in_specs=(
            P(("rep", "region", "dev"), None),
            P(("rep", "region", "dev"), None, None),
            P(("rep", "region", "dev"), None),
            P(("rep", "region", "dev")),
        ),
        out_specs=P(("rep", "region", "dev"), None),
        check_vma=False,
    )
```

```python
import functools

import jax
import jax.numpy as jnp
from jax import lax
from jax.experimental import pallas as pl
from jax.experimental.pallas import tpu as pltpu
from jax.sharding import PartitionSpec as P

ITERS = 3
REACH = 2
CHUNKS = 2
ROWS = 512
KINDS = REACH + 1

damping = 0.8

MESH = pl.DeviceIdType.MESH


def kernel(n, cols_ref, count_ref, tiles_hbm, q_ref, out_hbm, *scratch):
    slots, tile, _ = tiles_hbm.shape
    width = q_ref.shape[1] // CHUNKS
    steps = ITERS * CHUNKS
    tiles_ref, wt_ref = scratch[:2]
    srcs = scratch[2 : 2 + steps]
    gots = scratch[2 + steps : 2 + 2 * steps]
    puts = scratch[2 + 2 * steps : 2 + 3 * steps]
    sums = scratch[2 + 3 * steps : 2 + 3 * steps + CHUNKS]
    send_sem, recv_sem, tile_sem, out_sem = scratch[2 + 3 * steps + CHUNKS :]
    fetches = [
        pltpu.make_async_copy(tiles_hbm.at[s], tiles_ref.at[s], tile_sem.at[s])
        for s in range(slots)
    ]

    rep = lax.axis_index("rep")
    region = lax.axis_index("region")
    me = lax.axis_index("dev")

    bins, gates = [], []
    for s in range(slots):
        distance = cols_ref[0, s] - (region * n + me)
        live = s < count_ref[0]
        place = jnp.where(distance > REACH, REACH + 1, distance)
        bins.append(jnp.where(live, place, 0))
        alive = jnp.where(live, 1.0, 0.0).astype(jnp.float32)
        gates.append([jnp.where(place == k, alive, 0.0) for k in range(KINDS + 1)] + [alive])

    has_lower = [me >= d for d in range(1, REACH + 1)] + [region == 1]
    has_upper = [me + d < n for d in range(1, REACH + 1)] + [region == 0]
    lower = [(rep, region, me - d) for d in range(1, REACH + 1)] + [(rep, 0, me)]
    upper = [(rep, region, me + d) for d in range(1, REACH + 1)] + [(rep, 1, me)]

    for fetch in fetches:
        fetch.start()

    barrier = pltpu.get_barrier_semaphore()
    count = jnp.int32(0)
    for there, device in list(zip(has_lower, lower)) + list(zip(has_upper, upper)):
        count = count + there.astype(jnp.int32)

        @pl.when(there)
        def _(device=device):
            pl.semaphore_signal(barrier, inc=1, device_id=device, device_id_type=MESH)

    for ch in range(CHUNKS):
        srcs[ch][0] = q_ref[:, ch * width : (ch + 1) * width]
    pl.semaphore_wait(barrier, count)

    def field_copy(step, k, device):
        return pltpu.make_async_remote_copy(
            src_ref=srcs[step].at[0],
            dst_ref=srcs[step].at[k + 1],
            send_sem=send_sem.at[step, k],
            recv_sem=recv_sem.at[step, k],
            device_id=device,
            device_id_type=MESH,
        )

    def product_copy(step, k, device):
        return pltpu.make_async_remote_copy(
            src_ref=puts[step].at[k],
            dst_ref=gots[step].at[k],
            send_sem=send_sem.at[step, KINDS + k],
            recv_sem=recv_sem.at[step, KINDS + k],
            device_id=device,
            device_id_type=MESH,
        )

    def send_fields(step):
        for k in range(KINDS):

            @pl.when(has_lower[k])
            def _(k=k):
                field_copy(step, k, lower[k]).start()

    def send_products(step):
        source = srcs[step]

        @pl.loop(0, tile // ROWS)
        def _(i):
            rows = pl.ds(pl.multiple_of(i * ROWS, ROWS), ROWS)
            parts = [
                jnp.dot(wt_ref[s, rows, :], source[0], preferred_element_type=jnp.float32)
                for s in range(slots)
            ]
            for k in range(KINDS):
                total = gates[0][k + 1] * parts[0]
                for s in range(1, slots):
                    total = total + gates[s][k + 1] * parts[s]
                puts[step][k, rows, :] = total.astype(jnp.bfloat16)

        for k in range(KINDS):

            @pl.when(has_upper[k])
            def _(k=k):
                product_copy(step, k, upper[k]).start()

    def result_copy(ch):
        return pltpu.make_async_copy(
            sums[ch], out_hbm.at[:, pl.ds(ch * width, width)], out_sem.at[ch]
        )

    def finish(step):
        it, ch = divmod(step, CHUNKS)
        columns = pl.ds(ch * width, width)
        source = srcs[step]

        for k in range(KINDS):

            @pl.when(has_upper[k])
            def _(k=k):
                field_copy(step, k, upper[k]).wait_recv()

        @pl.loop(0, tile // ROWS)
        def _(i):
            rows = pl.ds(pl.multiple_of(i * ROWS, ROWS), ROWS)
            total = jnp.zeros((ROWS, width), jnp.float32)
            for s in range(slots):
                live = gates[s][KINDS + 1]
                total = total + live * jnp.dot(
                    tiles_ref[s, rows, :], source[bins[s]], preferred_element_type=jnp.float32
                )
            sums[ch][rows, :] = total

        for k in range(KINDS):

            @pl.when(has_lower[k])
            def _(k=k):
                product_copy(step, k, lower[k]).wait_recv()

        @pl.loop(0, tile // ROWS)
        def _(i):
            rows = pl.ds(pl.multiple_of(i * ROWS, ROWS), ROWS)
            total = sums[ch][rows, :]
            for k in range(KINDS):
                landed = gots[step][k, rows, :].astype(jnp.float32)
                total = total + jnp.where(has_lower[k], landed, jnp.zeros_like(landed))
            update = damping * total + q_ref[rows, columns].astype(jnp.float32)
            if it == ITERS - 1:
                sums[ch][rows, :] = update
            else:
                srcs[step + CHUNKS][0, rows, :] = update.astype(jnp.bfloat16)

        if it == ITERS - 1:
            result_copy(ch).start()

    for ch in range(CHUNKS):
        send_fields(ch)

    for s in range(slots):
        fetches[s].wait()

        @pl.loop(0, tile // ROWS)
        def _(i, s=s):
            rows = pl.ds(pl.multiple_of(i * ROWS, ROWS), ROWS)
            wt_ref[s, rows, :] = tiles_ref[s, :, rows].T

    for ch in range(CHUNKS):
        send_products(ch)

    for step in range(steps):
        finish(step)
        if step + CHUNKS < steps:
            send_fields(step + CHUNKS)
            send_products(step + CHUNKS)

    for step in range(steps):
        for k in range(KINDS):

            @pl.when(has_lower[k])
            def _(step=step, k=k):
                field_copy(step, k, lower[k]).wait_send()

            @pl.when(has_upper[k])
            def _(step=step, k=k):
                product_copy(step, k, upper[k]).wait_send()

    for ch in range(CHUNKS):
        result_copy(ch).wait()


def on_device(queries, tiles, tile_cols, tile_count):
    n = lax.axis_size("dev")
    slots, tile, _ = tiles.shape
    cols = queries.shape[1]
    width = cols // CHUNKS
    steps = ITERS * CHUNKS
    vmem = pl.BlockSpec(memory_space=pltpu.VMEM)
    smem = pl.BlockSpec(memory_space=pltpu.SMEM)
    products = 2 * slots * ITERS
    return pl.pallas_call(
        functools.partial(kernel, n),
        out_shape=jax.ShapeDtypeStruct((tile, cols), jnp.float32),
        in_specs=[smem, smem, pl.BlockSpec(memory_space=pl.ANY), vmem],
        out_specs=pl.BlockSpec(memory_space=pl.ANY),
        scratch_shapes=[pltpu.VMEM((slots, tile, tile), jnp.bfloat16)] * 2
        + [pltpu.VMEM((KINDS + 1, tile, width), jnp.bfloat16)] * steps
        + [pltpu.VMEM((KINDS, tile, width), jnp.bfloat16)] * (2 * steps)
        + [pltpu.VMEM((tile, width), jnp.float32)] * CHUNKS
        + [pltpu.SemaphoreType.DMA((steps, 2 * KINDS))] * 2
        + [pltpu.SemaphoreType.DMA((slots,)), pltpu.SemaphoreType.DMA((CHUNKS,))],
        compiler_params=pltpu.CompilerParams(
            collective_id=0, has_side_effects=True, vmem_limit_bytes=58 * 2**20
        ),
        cost_estimate=pl.CostEstimate(
            flops=2 * products * tile * tile * cols,
            bytes_accessed=2 * tiles.size + 6 * tile * cols,
            transcendentals=0,
        ),
        name="diffuse",
    )(tile_cols, tile_count, tiles, queries)


def solution(mesh):
    return jax.shard_map(
        on_device,
        mesh=mesh,
        in_specs=(
            P(("rep", "region", "dev"), None),
            P(("rep", "region", "dev"), None, None),
            P(("rep", "region", "dev"), None),
            P(("rep", "region", "dev")),
        ),
        out_specs=P(("rep", "region", "dev"), None),
        check_vma=False,
    )
```
